32 devices in a mesh: gx: 8 (over y, x, core), gy: 4 (over z).
Axes of the slice: x: 2, y: 2, z: 4, core: 2. Of those that a mesh axis runs over, the one named last changes fastest.
Arguments:
- east_blocks: int32 [16, 4], P(None, 'gy'), may hold values from 0 to 2, as said below
- job_code: int32 [200, 4], P('gx', 'gy'), may hold values from -1 to 554, as said below
- factor_panels: bfloat16 [200, 4, 2, 1536, 128], P('gx', 'gy'), as said below
- dual_rhs: float32 [16, 4, 256, 384], P('gx', 'gy'), may hold values from -6 to 6
Outputs:
- multipliers: float32 [16, 4, 256, 384], P('gx', 'gy')
- residual: float32 [16, 4, 256, 384], P('gx', 'gy')
The draws below stay inside these ranges and needn't reach their ends.
Inputs may be any that keep to these rules, and one draw needn't show every extreme that they name: `east_blocks`: in each row sy the faces sx = s0 to s0 + 3 carry 2 blocks, for a start s0 drawn per row from 1 to 10; the other faces carry 1, and the face at sx = 15 carries 0. `job_code`: A code (sx * 6 + bi) * 6 + bj names the upper tile bi <= bj < nb of subdomain (sx, sy) for column sy. In each column the live tiles, ordered by sx, then bi, then bj, are numbered k = 0, 1, ... and sit at row (k % 8) * 25 + k // 8; all other slots hold -1. Hence one device of gx forms at most 6 tiles of the subdomains of one gx index, and exactly 6 for some. `factor_panels`: A live slot holds column blocks bi and bj of subdomain (sx, sy)'s factor of 1536 rows and 768 columns, the same block wherever it appears; empty slots hold zeros.
All inputs are finite; a program needn't handle non-finite values.
Results may differ from the reference program's by a relative error of at most 0.0059.
Values may be sent and summed in bfloat16 or wider, within the bound.
A program may use at most 128 MiB of HBM per device.

```python
from functools import partial
import jax
import jax.numpy as jnp
from jax import lax

NB = 6
BLK = 128
KF = 1536
CASES = 256
ITERS = 4
SX = 16
SY = 4
BANDF = 4
FACE = 384
JOB_DEV = 25
N_GX = 8


def band_starts(key):
    return jax.random.randint(jax.random.fold_in(key, 11), (SY,), 1, SX - 1 - BANDF).astype(jnp.int32)


def face_blocks(key):
    starts = band_starts(key)
    face_index = jnp.arange(SX, dtype=jnp.int32)[:, None]
    is_heavy = (face_index >= starts[None, :]) & (face_index < starts[None, :] + BANDF)
    blocks = jnp.where(is_heavy, 2, 1).astype(jnp.int32)
    return jnp.where(face_index < SX - 1, blocks, 0).astype(jnp.int32)


def tile_table(key):
    east_part = face_blocks(key)
    west_part = jnp.concatenate([jnp.zeros((1, SY), jnp.int32), east_part[:-1]], axis=0)
    row_index = jnp.arange(SY, dtype=jnp.int32)[None, :]
    interface_blocks = west_part + east_part + (row_index > 0).astype(jnp.int32) + (row_index < SY - 1).astype(jnp.int32)
    all_codes = jnp.arange(SX * NB * NB, dtype=jnp.int32)
    owner_sx = all_codes // (NB * NB)
    first_block = all_codes % (NB * NB) // NB
    second = all_codes % NB
    is_live = (first_block <= second)[:, None] & (second[:, None] < interface_blocks[owner_sx])
    tile_order = jnp.cumsum(is_live.astype(jnp.int32), axis=0) - 1
    place_slots = tile_order % N_GX * JOB_DEV + tile_order // N_GX
    place_slots = jnp.where(is_live, place_slots, N_GX * JOB_DEV).astype(jnp.int32)
    column_ids = jnp.broadcast_to(jnp.arange(SY, dtype=jnp.int32)[None, :], is_live.shape)
    values = jnp.broadcast_to(all_codes[:, None], is_live.shape)
    code_table = jnp.full((N_GX * JOB_DEV, SY), -1, jnp.int32)
    return code_table.at[place_slots, column_ids].set(values, mode='drop')


def draw_east_blocks(key, part):
    return face_blocks(key)


def draw_job_code(key, part):
    return tile_table(key)


def draw_factor_panels(key, part):
    code_table = tile_table(key).reshape(-1)
    column_ids = jnp.arange(code_table.shape[0], dtype=jnp.int32) % SY
    base_key = jax.random.fold_in(key, 29)

    def one_slot(job_item):
        tile_code, column = job_item
        safe_code = jnp.maximum(tile_code, 0)
        owner_sx = safe_code // (NB * NB)
        first_block = safe_code % (NB * NB) // NB
        second = safe_code % NB

        def make_panel(block_index):
            panel_key = jax.random.fold_in(base_key, (owner_sx * SY + column) * NB + block_index)
            values = jax.random.normal(panel_key, (KF, BLK), jnp.float32)
            return values * KF ** (-0.5)
        panel_pair = jnp.stack([make_panel(first_block), make_panel(second)])
        return jnp.where(tile_code >= 0, panel_pair, 0.0).astype(jnp.bfloat16)
    panels = lax.map(one_slot, (code_table, column_ids))
    return panels.reshape(N_GX * JOB_DEV, SY, 2, KF, BLK)


def level_of(own_key, shape, split, smallest, top_value):
    level = 1.0
    for axis_at, parts in split:
        heights = jax.random.uniform(jax.random.fold_in(jax.random.fold_in(own_key, 6), axis_at), (parts,), jnp.float32, smallest / len(split), top_value / len(split))
        level = level * jnp.repeat(jnp.exp(heights), shape[axis_at] // parts).reshape((-1,) + (1,) * (len(shape) - 1 - axis_at))
    return level


def centred(stream_key, extent, spread, reach, split=(), kind=jnp.bfloat16):
    values = jax.random.normal(stream_key, extent, jnp.float32) * spread
    if len(split) > 0:
        values = level_of(stream_key, extent, split, -0.22, 0.18) * values
    return jnp.clip(values, min=-reach, max=reach).astype(kind)


def setup_inputs(seed: int = 0) -> dict:
    arg_keys = jax.random.split(jax.random.key(seed), 5)
    return {
        "east_blocks": draw_east_blocks(jax.random.fold_in(arg_keys[4], 71), 0),
        "job_code": draw_job_code(jax.random.fold_in(arg_keys[4], 71), 0),
        "factor_panels": draw_factor_panels(jax.random.fold_in(arg_keys[4], 71), 0),
        "dual_rhs": centred(arg_keys[3], (SX, SY, CASES, FACE), 1.0, 6.0, ((0, 8), (1, 4)), jnp.float32),
    }


CHEB_LOW = 0.2
CHEB_HIGH = 7.0


def block_mask(count, blocks, block_len):
    lane_block = jnp.arange(blocks * block_len, dtype=jnp.int32) // block_len
    return (lane_block < count).astype(jnp.float32)


def place_slots(west_part, east_part, south_part, north_part, counts, block_len):
    local_vec = jnp.zeros((west_part.shape[0], NB * block_len), jnp.float32)
    anchor = jnp.zeros((), jnp.int32)
    local_vec = lax.dynamic_update_slice(local_vec, west_part * block_mask(counts[0], 2, block_len), (anchor, anchor))
    local_vec = lax.dynamic_update_slice(local_vec, east_part * block_mask(counts[1], 2, block_len), (anchor, counts[0] * block_len))
    local_vec = lax.dynamic_update_slice(local_vec, south_part * block_mask(counts[2], 1, block_len), (anchor, (counts[0] + counts[1]) * block_len))
    local_vec = lax.dynamic_update_slice(local_vec, north_part * block_mask(counts[3], 1, block_len), (anchor, (counts[0] + counts[1] + counts[2]) * block_len))
    return local_vec


def read_slots(local_vec, counts, block_len):
    west_part = local_vec[:, :2 * block_len] * block_mask(counts[0], 2, block_len)
    east_part = lax.dynamic_slice_in_dim(local_vec, counts[0] * block_len, 2 * block_len, 1) * block_mask(counts[1], 2, block_len)
    south_part = lax.dynamic_slice_in_dim(local_vec, (counts[0] + counts[1]) * block_len, block_len, 1) * block_mask(counts[2], 1, block_len)
    north_part = lax.dynamic_slice_in_dim(local_vec, (counts[0] + counts[1] + counts[2]) * block_len, block_len, 1) * block_mask(counts[3], 1, block_len)
    return west_part, east_part, south_part, north_part


def place_all(west_part, east_part, south_part, north_part, counts, block_len):
    return jax.vmap(partial(place_slots, block_len=block_len))(west_part, east_part, south_part, north_part, counts)


def read_all(local_vec, counts, block_len):
    return jax.vmap(partial(read_slots, block_len=block_len))(local_vec, counts)


def symmetric(upper_tiles):
    upper_f = upper_tiles.astype(jnp.float32)
    flipped = jnp.swapaxes(jnp.swapaxes(upper_f, 1, 2), 3, 4)
    block_row = jnp.arange(NB, dtype=jnp.int32)
    keep_upper = (block_row[:, None] <= block_row[None, :])[None, :, :, None, None]
    full_tiles = jnp.where(keep_upper, upper_f, flipped)
    full_width = NB * upper_tiles.shape[3]
    return full_tiles.transpose(0, 1, 3, 2, 4).reshape(upper_tiles.shape[0], full_width, full_width)


def face_mask(counts, block_len):
    east_lane = jnp.arange(2 * block_len, dtype=jnp.int32) // block_len
    east_ok = east_lane < counts[..., 1:2]
    north_ok = jnp.zeros((block_len,), jnp.int32) < counts[..., 3:4]
    return jnp.concatenate([east_ok, north_ok], axis=-1).astype(jnp.float32)


def subdomain_counts(east_blocks):
    west_blocks = jnp.concatenate([jnp.zeros((1, SY), jnp.int32), east_blocks[:-1]], axis=0)
    row_index = jnp.arange(SY, dtype=jnp.int32)
    south_blocks = jnp.broadcast_to((row_index > 0).astype(jnp.int32)[None, :], (SX, SY))
    north_blocks = jnp.broadcast_to((row_index < SY - 1).astype(jnp.int32)[None, :], (SX, SY))
    return jnp.stack([west_blocks, east_blocks, south_blocks, north_blocks], axis=-1)


def job_tiles(factor_panels):
    grouped = factor_panels.reshape((N_GX, JOB_DEV) + factor_panels.shape[1:])

    def tiles_of(panel_group):
        left_panel = panel_group[:, :, 0].astype(jnp.float32)
        right_panel = panel_group[:, :, 1].astype(jnp.float32)
        return jnp.einsum("jyka,jykb->jyab", left_panel, right_panel, precision=lax.Precision.HIGHEST).astype(jnp.bfloat16)

    return lax.map(tiles_of, grouped).reshape((N_GX * JOB_DEV, SY, BLK, BLK))


def flatten(array):
    return array.reshape((SX * SY,) + array.shape[2:])


def apply_global(face_vec, matrices, flat_counts):
    east_part = face_vec[..., :2 * BLK]
    north_part = face_vec[..., 2 * BLK:]
    from_west = jnp.concatenate([jnp.zeros_like(east_part[:1]), east_part[:-1]], axis=0)
    from_south = jnp.concatenate([jnp.zeros_like(north_part[:, :1]), north_part[:, :-1]], axis=1)
    local_vec = place_all(flatten(-from_west), flatten(east_part), flatten(-from_south), flatten(north_part), flat_counts, BLK)
    image = jnp.einsum("ncm,nmk->nck", local_vec, matrices, precision=lax.Precision.HIGHEST)
    west_y, east_y, south_y, north_y = read_all(image, flat_counts, BLK)
    west_y = west_y.reshape(SX, SY, CASES, 2 * BLK)
    east_y = east_y.reshape(SX, SY, CASES, 2 * BLK)
    south_y = south_y.reshape(SX, SY, CASES, BLK)
    north_y = north_y.reshape(SX, SY, CASES, BLK)
    east_near = jnp.concatenate([west_y[1:], jnp.zeros_like(west_y[:1])], axis=0)
    north_near = jnp.concatenate([south_y[:, 1:], jnp.zeros_like(south_y[:, :1])], axis=1)
    return jnp.concatenate([east_y - east_near, north_y - north_near], axis=-1)


def reference(east_blocks, job_code, factor_panels, dual_rhs):
    counts = subdomain_counts(east_blocks)
    flat_counts = counts.reshape(SX * SY, 4)
    tiles = job_tiles(factor_panels)
    column_ids = jnp.broadcast_to(jnp.arange(SY, dtype=jnp.int32)[None, :], job_code.shape)
    target = jnp.where(job_code >= 0, job_code, SX * NB * NB).astype(jnp.int32)
    upper_tiles = jnp.zeros((SX * NB * NB, SY, BLK, BLK), jnp.bfloat16).at[target, column_ids].set(tiles, mode="drop")
    upper_tiles = upper_tiles.reshape(SX, NB, NB, SY, BLK, BLK).transpose(0, 3, 1, 2, 4, 5).reshape(SX * SY, NB, NB, BLK, BLK)
    matrices = lax.map(lambda single: symmetric(single[None])[0], upper_tiles)
    face_ok = face_mask(counts, BLK)[:, :, None, :]
    residual = dual_rhs * face_ok
    cheb_center = (CHEB_HIGH + CHEB_LOW) / 2.0
    cheb_radius = (CHEB_HIGH - CHEB_LOW) / 2.0
    cheb_ratio = cheb_center / cheb_radius
    cheb_rho = 1.0 / cheb_ratio
    update = residual / cheb_center
    multipliers = jnp.zeros_like(residual)
    for sweep in range(ITERS):
        multipliers = multipliers + update
        residual = residual - apply_global(update, matrices, flat_counts)
        rho_next = 1.0 / (2.0 * cheb_ratio - cheb_rho)
        update = (rho_next * cheb_rho) * update + (2.0 * rho_next / cheb_radius) * residual
        cheb_rho = rho_next
    return multipliers, residual
```

```python
import functools

import jax
import jax.numpy as jnp
from jax import lax
from jax.experimental import pallas as pl
from jax.experimental.pallas import tpu as pltpu
from jax.sharding import PartitionSpec as P

NB = 6
ITERS = 4
CHEB_LOW = 0.2
CHEB_HIGH = 7.0
MESH = pl.DeviceIdType.MESH
F32 = jnp.float32
BF16 = jnp.bfloat16


def upper_count(blocks):
    return blocks * (blocks + 1) // 2


def kernel(
    gx_n, gy_n, jobs, subs, cap, blk,
    east_ref, panels_ref, rhs_ref, mult_ref, res_ref,
    panels, tiles, send_buf, got, mats, x_ref, r_ref, y_ref, xb_ref,
    rw, re, rs, rn, sw, se, ss, sn, iw, isou,
    first_tile, panel_sem, tile_send, tile_recv, face_send, face_recv, init_send, init_recv,
):
    gx = lax.axis_index("gx")
    gy = lax.axis_index("gy")
    rows = rhs_ref.shape[2]
    two = 2 * blk
    south_n = (gy > 0).astype(jnp.int32)
    north_n = (gy < gy_n - 1).astype(jnp.int32)

    def panel_copy(j):
        return pltpu.make_async_copy(panels_ref.at[j, 0], panels.at[j], panel_sem.at[j])

    for j in range(jobs):
        panel_copy(j).start()

    @pl.when(gx == 0)
    def _():
        rw[...] = jnp.zeros_like(rw)
        iw[...] = jnp.zeros_like(iw)

    @pl.when(gx == gx_n - 1)
    def _():
        re[...] = jnp.zeros_like(re)

    @pl.when(gy == 0)
    def _():
        rs[...] = jnp.zeros_like(rs)
        isou[...] = jnp.zeros_like(isou)

    @pl.when(gy == gy_n - 1)
    def _():
        rn[...] = jnp.zeros_like(rn)

    barrier = pltpu.get_barrier_semaphore()

    @pl.loop(1, gx_n)
    def _(i):
        pl.semaphore_signal(barrier, inc=1, device_id=(lax.rem(gx + i, gx_n), gy), device_id_type=MESH)

    @pl.when(gy > 0)
    def _():
        pl.semaphore_signal(barrier, inc=1, device_id=(gx, gy - 1), device_id_type=MESH)

    @pl.when(gy < gy_n - 1)
    def _():
        pl.semaphore_signal(barrier, inc=1, device_id=(gx, gy + 1), device_id_type=MESH)

    pl.semaphore_wait(barrier, gx_n - 1 + south_n + north_n)

    def remote(src, dst, send, recv, dgx, dgy):
        return pltpu.make_async_remote_copy(
            src_ref=src, dst_ref=dst, send_sem=send, recv_sem=recv,
            device_id=(dgx, dgy), device_id_type=MESH,
        )

    has_w, has_e, has_s, has_n = gx > 0, gx < gx_n - 1, gy > 0, gy < gy_n - 1
    gxm, gxp = jnp.maximum(gx - 1, 0), jnp.minimum(gx + 1, gx_n - 1)
    gym, gyp = jnp.maximum(gy - 1, 0), jnp.minimum(gy + 1, gy_n - 1)

    init_e = remote(rhs_ref.at[subs - 1, 0, :, pl.ds(0, two)], iw, init_send.at[0], init_recv.at[0], gxp, gy)
    init_n = remote(rhs_ref.at[:, 0, :, pl.ds(two, blk)], isou, init_send.at[1], init_recv.at[1], gx, gyp)
    pl.when(has_e)(lambda: init_e.start())
    pl.when(has_n)(lambda: init_n.start())

    total = jnp.int32(0)
    before = jnp.int32(0)

    def count_step(i, carry):
        total, west = carry
        first_tile[i] = total
        east = east_ref[i, 0]
        return total + upper_count(west + east + south_n + north_n), east

    lax.fori_loop(0, gx_n * subs, count_step, (total, before))

    @pl.loop(0, jobs)
    def _(j):
        panel_copy(j).wait()
        tiles[j] = lax.dot_general(
            panels[j, 0], panels[j, 1], (((0,), (0,)), ((), ())), preferred_element_type=F32
        ).astype(BF16)

    def tile_copy(d, i, src):
        return remote(
            send_buf.at[pl.ds(d * cap, cap)], got.at[pl.ds(src * cap, cap)],
            tile_send.at[i], tile_recv.at[i], d, gy,
        )

    def slot_of(d, q):
        slot = (first_tile[d * subs] + gx_n * q - gx + gx_n - 1) // gx_n
        return jnp.clip(slot, 0, jobs - 1)

    @pl.loop(1, gx_n)
    def _(i):
        d = lax.rem(gx + i, gx_n)
        for q in range(cap):
            send_buf[d * cap + q] = tiles[slot_of(d, q)]
        tile_copy(d, i, gx).start()

    for q in range(cap):
        got[gx * cap + q] = tiles[slot_of(gx, q)]

    lane_w = lax.broadcasted_iota(jnp.int32, (1, two), 1) // blk

    def east_at(i):
        return east_ref[gx * subs + i, 0]

    def west_at(i):
        left = east_ref[jnp.maximum(gx * subs + i - 1, 0), 0]
        return left if i > 0 else jnp.where(gx > 0, left, 0)

    masks = []
    for s in range(subs):
        mask_w = (lane_w < west_at(s)).astype(F32)
        mask_e = (lane_w < east_at(s)).astype(F32)
        mask_s = jnp.zeros((1, blk), F32) + south_n.astype(F32)
        mask_n = jnp.zeros((1, blk), F32) + north_n.astype(F32)
        masks.append((mask_w, mask_e, mask_s, mask_n))
    lanes = ((0, two), (two, two), (2 * two, blk), (2 * two + blk, blk))

    center = (CHEB_HIGH + CHEB_LOW) / 2.0
    radius = (CHEB_HIGH - CHEB_LOW) / 2.0
    ratio = center / radius
    rho = 1.0 / ratio

    pl.when(has_w)(lambda: init_e.wait_recv())
    pl.when(has_s)(lambda: init_n.wait_recv())
    pl.when(has_e)(lambda: init_e.wait_send())
    pl.when(has_n)(lambda: init_n.wait_send())
    step = 64

    @pl.loop(0, rows // step)
    def _(c):
        rr = pl.ds(c * step, step)
        for s in range(subs):
            west = -iw[rr, :] if s == 0 else -rhs_ref[s - 1, 0, rr, 0:two]
            parts = (west, rhs_ref[s, 0, rr, 0:two], -isou[s, rr, :], rhs_ref[s, 0, rr, two:two + blk])
            for g, (lo, width) in enumerate(lanes):
                r = parts[g] * masks[s][g]
                u = r / center
                r_ref[s, rr, lo:lo + width] = r
                x_ref[s, rr, lo:lo + width] = u
                xb_ref[s, rr, lo:lo + width] = u.astype(BF16)
                if g == 1:
                    mult_ref[s, 0, rr, 0:two] = u
                if g == 3:
                    mult_ref[s, 0, rr, two:two + blk] = u

    @pl.loop(1, gx_n)
    def _(i):
        copy = tile_copy(lax.rem(gx + i, gx_n), i, gx)
        copy.wait()

    base = first_tile[gx * subs]
    for s in range(subs):
        west, east = west_at(s), east_at(s)
        nb = west + east + south_n + north_n
        limit = NB - 1
        place = [jnp.int32(0), jnp.int32(1), west, west + 1, west + east, west + east + south_n]
        place = [jnp.minimum(p, limit) for p in place]
        for a in range(NB):
            for b in range(a, NB):
                pa, pb = place[a], place[b]
                k = first_tile[gx * subs + s] + pa * nb - pa * (pa - 1) // 2 + pb - pa
                k = jnp.clip(k, base, base + cap * gx_n - 1)
                tile = got[lax.rem(k, gx_n) * cap + (k - base) // gx_n]
                mats[s, a * blk:(a + 1) * blk, b * blk:(b + 1) * blk] = tile
                if a < b:
                    mats[s, b * blk:(b + 1) * blk, a * blk:(a + 1) * blk] = tile.T

    for t in range(ITERS):
        last = t == ITERS - 1

        def product(s, g):
            lo, width = lanes[g]
            return jnp.dot(xb_ref[s], mats[s, :, lo:lo + width], preferred_element_type=F32)

        to_w = remote(sw.at[t], re.at[t], face_send.at[t, 0], face_recv.at[t, 0], gxm, gy)
        to_e = remote(se.at[t], rw.at[t], face_send.at[t, 1], face_recv.at[t, 1], gxp, gy)
        to_s = remote(ss.at[t], rn.at[t], face_send.at[t, 2], face_recv.at[t, 2], gx, gym)
        to_n = remote(sn.at[t], rs.at[t], face_send.at[t, 3], face_recv.at[t, 3], gx, gyp)
        copies = [(to_s, has_s, has_n), (to_w, has_w, has_e)]
        if not last:
            copies += [(to_n, has_n, has_s), (to_e, has_e, has_w)]

        for s in range(subs):
            y = product(s, 2)
            y_ref[s, :, 2 * two:2 * two + blk] = y
            ss[t, s] = y.astype(BF16)
        pl.when(has_s)(to_s.start)
        for s in range(subs):
            y = product(s, 3)
            y_ref[s, :, 2 * two + blk:] = y
            if not last:
                sn[t, s] = y.astype(BF16)
        if not last:
            pl.when(has_n)(to_n.start)
        y = product(0, 0)
        y_ref[0, :, 0:two] = y
        sw[t] = y.astype(BF16)
        pl.when(has_w)(to_w.start)
        y = product(subs - 1, 1)
        y_ref[subs - 1, :, two:2 * two] = y
        if not last:
            se[t] = y.astype(BF16)
            pl.when(has_e)(to_e.start)
        for s in range(subs):
            if s > 0:
                y_ref[s, :, 0:two] = product(s, 0)
            if s < subs - 1:
                y_ref[s, :, two:2 * two] = product(s, 1)

        for copy, sends, receives in copies:
            pl.when(receives)(copy.wait_recv)
            pl.when(sends)(copy.wait_send)

        rho_next = 1.0 / (2.0 * ratio - rho)
        keep, gain = rho_next * rho, 2.0 * rho_next / radius
        rho = rho_next

        @pl.loop(0, rows // step)
        def _(c):
            rr = pl.ds(c * step, step)
            for s in range(subs):
                for g, (lo, width) in enumerate(lanes):
                    if last and g in (0, 2):
                        continue
                    if g == 0:
                        other = rw[t, rr, :].astype(F32) if s == 0 else y_ref[s - 1, rr, two:2 * two]
                    elif g == 1:
                        other = re[t, rr, :].astype(F32) if s == subs - 1 else y_ref[s + 1, rr, 0:two]
                    elif g == 2:
                        other = rs[t, s, rr, :].astype(F32)
                    else:
                        other = rn[t, s, rr, :].astype(F32)
                    y = y_ref[s, rr, lo:lo + width]
                    r = r_ref[s, rr, lo:lo + width] - (y - other) * masks[s][g]
                    olo, ohi = (0, two) if g == 1 else (two, two + blk)
                    if last:
                        res_ref[s, 0, rr, olo:ohi] = r
                        continue
                    u = keep * x_ref[s, rr, lo:lo + width] + gain * r
                    r_ref[s, rr, lo:lo + width] = r
                    x_ref[s, rr, lo:lo + width] = u
                    xb_ref[s, rr, lo:lo + width] = u.astype(BF16)
                    if g in (1, 3):
                        mult_ref[s, 0, rr, olo:ohi] = mult_ref[s, 0, rr, olo:ohi] + u


def shards(gx_n, gy_n, east_blocks, job_code, factor_panels, dual_rhs):
    jobs = factor_panels.shape[0]
    depth, blk = factor_panels.shape[-2:]
    subs, _, rows, face = dual_rhs.shape
    cap = (subs * upper_count(NB) + gx_n - 1) // gx_n
    width = NB * blk
    vm = pltpu.VMEM
    dma = pltpu.SemaphoreType.DMA
    half = (ITERS, rows, 2 * blk)
    pair = (ITERS, subs, rows, blk)
    out = jax.ShapeDtypeStruct(dual_rhs.shape, F32)
    return pl.pallas_call(
        functools.partial(kernel, gx_n, gy_n, jobs, subs, cap, blk),
        out_shape=(out, out),
        in_specs=[
            pl.BlockSpec(memory_space=pltpu.SMEM),
            pl.BlockSpec(memory_space=pl.ANY),
            pl.BlockSpec(memory_space=vm),
        ],
        out_specs=(pl.BlockSpec(memory_space=vm), pl.BlockSpec(memory_space=vm)),
        scratch_shapes=[
            vm((jobs, 2, depth, blk), BF16),
            vm((jobs, blk, blk), BF16),
            vm((gx_n * cap, blk, blk), BF16),
            vm((gx_n * cap, blk, blk), BF16),
            vm((subs, width, width), BF16),
            vm((subs, rows, width), F32),
            vm((subs, rows, width), F32),
            vm((subs, rows, width), F32),
            vm((subs, rows, width), BF16),
            vm(half, BF16), vm(half, BF16), vm(pair, BF16), vm(pair, BF16),
            vm(half, BF16), vm(half, BF16), vm(pair, BF16), vm(pair, BF16),
            vm((rows, 2 * blk), F32),
            vm((subs, rows, blk), F32),
            pltpu.SMEM((gx_n * subs,), jnp.int32),
            dma((jobs,)), dma((gx_n,)), dma((gx_n,)),
            dma((ITERS, 4)), dma((ITERS, 4)), dma((2,)), dma((2,)),
        ],
        compiler_params=pltpu.CompilerParams(
            collective_id=0, has_side_effects=True, vmem_limit_bytes=56 * 2**20
        ),
    )(east_blocks, factor_panels, dual_rhs)


def solution(mesh):
    in_specs = (
        P(None, "gy"),
        P("gx", "gy"),
        P("gx", "gy", None, None, None),
        P("gx", "gy", None, None),
    )
    out_specs = (P("gx", "gy", None, None), P("gx", "gy", None, None))
    body = functools.partial(shards, mesh.shape["gx"], mesh.shape["gy"])
    return jax.shard_map(body, mesh=mesh, in_specs=in_specs, out_specs=out_specs, check_vma=False)
```

```python
import functools

import jax
import jax.numpy as jnp
from jax import lax
from jax.experimental import pallas as pl
from jax.experimental.pallas import tpu as pltpu
from jax.sharding import PartitionSpec as P

NB = 6
ITERS = 4
HALVES = 2
CHEB_LOW = 0.2
CHEB_HIGH = 7.0
MESH = pl.DeviceIdType.MESH
F32 = jnp.float32
BF16 = jnp.bfloat16


def upper_count(blocks):
    return blocks * (blocks + 1) // 2


def kernel(
    gx_n, gy_n, jobs, subs, cap, blk,
    east_ref, panels_ref, rhs_ref, mult_ref, res_ref,
    panels, tiles, send_buf, got, mats, x_ref, r_ref, y_ref, xb_ref,
    rw, re, rs, rn, sw, se, ss, sn, iw, isou,
    first_tile, panel_sem, tile_send, tile_recv, face_send, face_recv, init_send, init_recv,
):
    gx = lax.axis_index("gx")
    gy = lax.axis_index("gy")
    rows = rhs_ref.shape[2]
    two = 2 * blk
    south_n = (gy > 0).astype(jnp.int32)
    north_n = (gy < gy_n - 1).astype(jnp.int32)

    def panel_copy(j):
        return pltpu.make_async_copy(panels_ref.at[j, 0], panels.at[j], panel_sem.at[j])

    for j in range(jobs):
        panel_copy(j).start()

    @pl.when(gx == 0)
    def _():
        rw[...] = jnp.zeros_like(rw)
        iw[...] = jnp.zeros_like(iw)

    @pl.when(gx == gx_n - 1)
    def _():
        re[...] = jnp.zeros_like(re)

    @pl.when(gy == 0)
    def _():
        rs[...] = jnp.zeros_like(rs)
        isou[...] = jnp.zeros_like(isou)

    @pl.when(gy == gy_n - 1)
    def _():
        rn[...] = jnp.zeros_like(rn)

    barrier = pltpu.get_barrier_semaphore()

    @pl.loop(1, gx_n)
    def _(i):
        pl.semaphore_signal(barrier, inc=1, device_id=(lax.rem(gx + i, gx_n), gy), device_id_type=MESH)

    @pl.when(gy > 0)
    def _():
        pl.semaphore_signal(barrier, inc=1, device_id=(gx, gy - 1), device_id_type=MESH)

    @pl.when(gy < gy_n - 1)
    def _():
        pl.semaphore_signal(barrier, inc=1, device_id=(gx, gy + 1), device_id_type=MESH)

    pl.semaphore_wait(barrier, gx_n - 1 + south_n + north_n)

    def remote(src, dst, send, recv, dgx, dgy):
        return pltpu.make_async_remote_copy(
            src_ref=src, dst_ref=dst, send_sem=send, recv_sem=recv,
            device_id=(dgx, dgy), device_id_type=MESH,
        )

    has_w, has_e, has_s, has_n = gx > 0, gx < gx_n - 1, gy > 0, gy < gy_n - 1
    gxm, gxp = jnp.maximum(gx - 1, 0), jnp.minimum(gx + 1, gx_n - 1)
    gym, gyp = jnp.maximum(gy - 1, 0), jnp.minimum(gy + 1, gy_n - 1)

    init_e = remote(rhs_ref.at[subs - 1, 0, :, pl.ds(0, two)], iw, init_send.at[0], init_recv.at[0], gxp, gy)
    init_n = remote(rhs_ref.at[:, 0, :, pl.ds(two, blk)], isou, init_send.at[1], init_recv.at[1], gx, gyp)
    pl.when(has_e)(lambda: init_e.start())
    pl.when(has_n)(lambda: init_n.start())

    total = jnp.int32(0)
    before = jnp.int32(0)

    def count_step(i, carry):
        total, west = carry
        first_tile[i] = total
        east = east_ref[0, i]
        return total + upper_count(west + east + south_n + north_n), east

    total, _ = lax.fori_loop(0, gx_n * subs, count_step, (total, before))
    first_tile[gx_n * subs] = total

    @pl.loop(0, jobs)
    def _(j):
        panel_copy(j).wait()
        tiles[j] = lax.dot_general(
            panels[j, 0], panels[j, 1], (((0,), (0,)), ((), ())), preferred_element_type=F32
        ).astype(BF16)

    def tile_copy(d, i, src):
        return remote(
            send_buf.at[pl.ds(d * cap, cap)], got.at[pl.ds(src * cap, cap)],
            tile_send.at[i], tile_recv.at[i], d, gy,
        )

    def slot_of(d, q):
        slot = (first_tile[d * subs] + gx_n * q - gx + gx_n - 1) // gx_n
        final = (first_tile[d * subs + subs] + gx_n - 1 - gx) // gx_n - 1
        return jnp.clip(jnp.minimum(slot, final), 0, jobs - 1)

    @pl.loop(1, gx_n)
    def _(i):
        d = lax.rem(gx + i, gx_n)
        for q in range(cap):
            send_buf[d * cap + q] = tiles[slot_of(d, q)]
        tile_copy(d, i, gx).start()

    for q in range(cap):
        got[gx * cap + q] = tiles[slot_of(gx, q)]

    lane_w = lax.broadcasted_iota(jnp.int32, (1, two), 1) // blk

    def east_at(i):
        return east_ref[0, gx * subs + i]

    def west_at(i):
        left = east_ref[0, jnp.maximum(gx * subs + i - 1, 0)]
        return left if i > 0 else jnp.where(gx > 0, left, 0)

    masks = []
    for s in range(subs):
        mask_w = (lane_w < west_at(s)).astype(F32)
        mask_e = (lane_w < east_at(s)).astype(F32)
        mask_s = jnp.zeros((1, blk), F32) + south_n.astype(F32)
        mask_n = jnp.zeros((1, blk), F32) + north_n.astype(F32)
        masks.append((mask_w, mask_e, mask_s, mask_n))
    lanes = ((0, two), (two, two), (2 * two, blk), (2 * two + blk, blk))

    center = (CHEB_HIGH + CHEB_LOW) / 2.0
    radius = (CHEB_HIGH - CHEB_LOW) / 2.0
    ratio = center / radius
    rho = 1.0 / ratio

    pl.when(has_w)(lambda: init_e.wait_recv())
    pl.when(has_s)(lambda: init_n.wait_recv())
    pl.when(has_e)(lambda: init_e.wait_send())
    pl.when(has_n)(lambda: init_n.wait_send())
    step = 64

    @pl.loop(0, rows // step)
    def _(c):
        rr = pl.ds(c * step, step)
        for s in range(subs):
            west = -iw[rr, :] if s == 0 else -rhs_ref[s - 1, 0, rr, 0:two]
            parts = (west, rhs_ref[s, 0, rr, 0:two], -isou[s, rr, :], rhs_ref[s, 0, rr, two:two + blk])
            for g, (lo, width) in enumerate(lanes):
                r = parts[g] * masks[s][g]
                u = r / center
                r_ref[s, rr, lo:lo + width] = r
                x_ref[s, rr, lo:lo + width] = u
                xb_ref[s, rr, lo:lo + width] = u.astype(BF16)
                if g == 1:
                    mult_ref[s, 0, rr, 0:two] = u
                if g == 3:
                    mult_ref[s, 0, rr, two:two + blk] = u

    @pl.loop(1, gx_n)
    def _(i):
        copy = tile_copy(lax.rem(gx + i, gx_n), i, gx)
        copy.wait()

    base, end = first_tile[gx * subs], first_tile[gx * subs + subs]
    for s in range(subs):
        west, east = west_at(s), east_at(s)
        nb = west + east + south_n + north_n
        limit = NB - 1
        place = [jnp.int32(0), jnp.int32(1), west, west + 1, west + east, west + east + south_n]
        place = [jnp.minimum(p, limit) for p in place]
        for a in range(NB):
            for b in range(a, NB):
                pa, pb = place[a], place[b]
                k = first_tile[gx * subs + s] + pa * nb - pa * (pa - 1) // 2 + pb - pa
                k = jnp.clip(k, base, end - 1)
                tile = got[lax.rem(k, gx_n) * cap + (k - base) // gx_n]
                mats[s, a * blk:(a + 1) * blk, b * blk:(b + 1) * blk] = tile
                if a < b:
                    mats[s, b * blk:(b + 1) * blk, a * blk:(a + 1) * blk] = tile.T

    part = rows // HALVES

    def product(h, s, g):
        lo, width = lanes[g]
        return jnp.dot(
            xb_ref[s, h * part:(h + 1) * part, :], mats[s, :, lo:lo + width], preferred_element_type=F32
        )

    def halo(t, h):
        sems = lambda g: (face_send.at[t, h, g], face_recv.at[t, h, g])
        to_s = remote(ss.at[t, h], rn.at[t, h], *sems(2), gx, gym), has_s, has_n
        to_w = remote(sw.at[t, h], re.at[t, h], *sems(0), gxm, gy), has_w, has_e
        if t == ITERS - 1:
            return to_s, to_w
        to_n = remote(sn.at[t, h], rs.at[t, h], *sems(3), gx, gyp), has_n, has_s
        to_e = remote(se.at[t, h], rw.at[t, h], *sems(1), gxp, gy), has_e, has_w
        return to_s, to_w, to_n, to_e

    def multiply(t, h):
        copies = halo(t, h)
        last = t == ITERS - 1
        rr = slice(h * part, (h + 1) * part)
        for s in range(subs):
            y = product(h, s, 2)
            y_ref[s, rr, 2 * two:2 * two + blk] = y
            ss[t, h, s] = y.astype(BF16)
        pl.when(has_s)(copies[0][0].start)
        for s in range(subs):
            y = product(h, s, 3)
            y_ref[s, rr, 2 * two + blk:] = y
            if not last:
                sn[t, h, s] = y.astype(BF16)
        if not last:
            pl.when(has_n)(copies[2][0].start)
        y = product(h, 0, 0)
        y_ref[0, rr, 0:two] = y
        sw[t, h] = y.astype(BF16)
        pl.when(has_w)(copies[1][0].start)
        y = product(h, subs - 1, 1)
        y_ref[subs - 1, rr, two:2 * two] = y
        if not last:
            se[t, h] = y.astype(BF16)
            pl.when(has_e)(copies[3][0].start)
        for s in range(subs):
            if s > 0:
                y_ref[s, rr, 0:two] = product(h, s, 0)
            if s < subs - 1:
                y_ref[s, rr, two:2 * two] = product(h, s, 1)

    def advance(t, h, keep, gain):
        last = t == ITERS - 1
        for copy, sends, receives in halo(t, h):
            pl.when(receives)(copy.wait_recv)
            pl.when(sends)(copy.wait_send)

        @pl.loop(0, part // step)
        def _(c):
            ll = pl.ds(c * step, step)
            rr = pl.ds(h * part + c * step, step)
            for s in range(subs):
                for g, (lo, width) in enumerate(lanes):
                    if last and g in (0, 2):
                        continue
                    if g == 0:
                        other = rw[t, h, ll, :].astype(F32) if s == 0 else y_ref[s - 1, rr, two:2 * two]
                    elif g == 1:
                        other = re[t, h, ll, :].astype(F32) if s == subs - 1 else y_ref[s + 1, rr, 0:two]
                    elif g == 2:
                        other = rs[t, h, s, ll, :].astype(F32)
                    else:
                        other = rn[t, h, s, ll, :].astype(F32)
                    y = y_ref[s, rr, lo:lo + width]
                    r = r_ref[s, rr, lo:lo + width] - (y - other) * masks[s][g]
                    olo, ohi = (0, two) if g == 1 else (two, two + blk)
                    if last:
                        res_ref[s, 0, rr, olo:ohi] = r
                        continue
                    u = keep * x_ref[s, rr, lo:lo + width] + gain * r
                    r_ref[s, rr, lo:lo + width] = r
                    x_ref[s, rr, lo:lo + width] = u
                    xb_ref[s, rr, lo:lo + width] = u.astype(BF16)
                    if g in (1, 3):
                        mult_ref[s, 0, rr, olo:ohi] = mult_ref[s, 0, rr, olo:ohi] + u

    for h in range(HALVES):
        multiply(0, h)
    for t in range(ITERS):
        rho_next = 1.0 / (2.0 * ratio - rho)
        keep, gain = rho_next * rho, 2.0 * rho_next / radius
        rho = rho_next
        for h in range(HALVES):
            advance(t, h, keep, gain)
            if t < ITERS - 1:
                multiply(t + 1, h)


def finish(mult_in, res_in, mult_out, res_out, sems):
    copies = [
        pltpu.make_async_copy(mult_in, mult_out, sems.at[0]),
        pltpu.make_async_copy(res_in, res_out, sems.at[1]),
    ]
    for copy in copies:
        copy.start()
    for copy in copies:
        copy.wait()


def shards(gx_n, gy_n, east_blocks, job_code, factor_panels, dual_rhs):
    jobs = factor_panels.shape[0]
    depth, blk = factor_panels.shape[-2:]
    subs, _, rows, face = dual_rhs.shape
    cap = (subs * upper_count(NB) + gx_n - 1) // gx_n
    width = NB * blk
    vm = pltpu.VMEM
    dma = pltpu.SemaphoreType.DMA
    half = (ITERS, HALVES, rows // HALVES, 2 * blk)
    pair = (ITERS, HALVES, subs, rows // HALVES, blk)
    out = jax.ShapeDtypeStruct(dual_rhs.shape, F32)
    mult, res = pl.pallas_call(
        functools.partial(kernel, gx_n, gy_n, jobs, subs, cap, blk),
        out_shape=(out, out),
        in_specs=[
            pl.BlockSpec(memory_space=pltpu.SMEM),
            pl.BlockSpec(memory_space=pl.ANY),
            pl.BlockSpec(memory_space=vm),
        ],
        out_specs=(pl.BlockSpec(memory_space=vm), pl.BlockSpec(memory_space=vm)),
        scratch_shapes=[
            vm((jobs, 2, depth, blk), BF16),
            vm((jobs, blk, blk), BF16),
            vm((gx_n * cap, blk, blk), BF16),
            vm((gx_n * cap, blk, blk), BF16),
            vm((subs, width, width), BF16),
            vm((subs, rows, width), F32),
            vm((subs, rows, width), F32),
            vm((subs, rows, width), F32),
            vm((subs, rows, width), BF16),
            vm(half, BF16), vm(half, BF16), vm(pair, BF16), vm(pair, BF16),
            vm(half, BF16), vm(half, BF16), vm(pair, BF16), vm(pair, BF16),
            vm((rows, 2 * blk), F32),
            vm((subs, rows, blk), F32),
            pltpu.SMEM((gx_n * subs + 1,), jnp.int32),
            dma((jobs,)), dma((gx_n,)), dma((gx_n,)),
            dma((ITERS, HALVES, 4)), dma((ITERS, HALVES, 4)), dma((2,)), dma((2,)),
        ],
        compiler_params=pltpu.CompilerParams(
            collective_id=0, has_side_effects=True, vmem_limit_bytes=56 * 2**20
        ),
    )(east_blocks.T, factor_panels, dual_rhs)
    anywhere = pl.BlockSpec(memory_space=pl.ANY)
    return pl.pallas_call(
        finish,
        out_shape=(out, out),
        in_specs=[anywhere, anywhere],
        out_specs=(anywhere, anywhere),
        scratch_shapes=[dma((2,))],
    )(mult, res)


def solution(mesh):
    in_specs = (
        P(None, "gy"),
        P("gx", "gy"),
        P("gx", "gy", None, None, None),
        P("gx", "gy", None, None),
    )
    out_specs = (P("gx", "gy", None, None), P("gx", "gy", None, None))
    body = functools.partial(shards, mesh.shape["gx"], mesh.shape["gy"])
    return jax.shard_map(body, mesh=mesh, in_specs=in_specs, out_specs=out_specs, check_vma=False)
```

```python
import functools

import jax
import jax.numpy as jnp
from jax import lax
from jax.experimental import pallas as pl
from jax.experimental.pallas import tpu as pltpu
from jax.sharding import PartitionSpec as P

NB = 6
ITERS = 4
HALVES = 2
CHEB_LOW = 0.2
CHEB_HIGH = 7.0
MESH = pl.DeviceIdType.MESH
F32 = jnp.float32
BF16 = jnp.bfloat16


def upper_count(blocks):
    return blocks * (blocks + 1) // 2


def kernel(
    gx_n, gy_n, jobs, subs, cap, blk,
    east_ref, panels_ref, rhs_ref, mult_ref, res_ref,
    panels, tiles, send_buf, got, mats, x_ref, r_ref, y_ref, xb_ref,
    rw, re, rs, rn, sw, se, ss, sn, iw, isou,
    first_tile, panel_sem, tile_send, tile_recv, face_send, face_recv, init_send, init_recv,
):
    gx = lax.axis_index("gx")
    gy = lax.axis_index("gy")
    rows = rhs_ref.shape[2]
    two = 2 * blk
    south_n = (gy > 0).astype(jnp.int32)
    north_n = (gy < gy_n - 1).astype(jnp.int32)

    def panel_copy(j):
        return pltpu.make_async_copy(panels_ref.at[j, 0], panels.at[j], panel_sem.at[j])

    for j in range(jobs):
        panel_copy(j).start()

    @pl.when(gx == 0)
    def _():
        rw[...] = jnp.zeros_like(rw)
        iw[...] = jnp.zeros_like(iw)

    @pl.when(gx == gx_n - 1)
    def _():
        re[...] = jnp.zeros_like(re)

    @pl.when(gy == 0)
    def _():
        rs[...] = jnp.zeros_like(rs)
        isou[...] = jnp.zeros_like(isou)

    @pl.when(gy == gy_n - 1)
    def _():
        rn[...] = jnp.zeros_like(rn)

    barrier = pltpu.get_barrier_semaphore()

    @pl.loop(1, gx_n)
    def _(i):
        pl.semaphore_signal(barrier, inc=1, device_id=(lax.rem(gx + i, gx_n), gy), device_id_type=MESH)

    @pl.when(gy > 0)
    def _():
        pl.semaphore_signal(barrier, inc=1, device_id=(gx, gy - 1), device_id_type=MESH)

    @pl.when(gy < gy_n - 1)
    def _():
        pl.semaphore_signal(barrier, inc=1, device_id=(gx, gy + 1), device_id_type=MESH)

    pl.semaphore_wait(barrier, gx_n - 1 + south_n + north_n)

    def remote(src, dst, send, recv, dgx, dgy):
        return pltpu.make_async_remote_copy(
            src_ref=src, dst_ref=dst, send_sem=send, recv_sem=recv,
            device_id=(dgx, dgy), device_id_type=MESH,
        )

    has_w, has_e, has_s, has_n = gx > 0, gx < gx_n - 1, gy > 0, gy < gy_n - 1
    gxm, gxp = jnp.maximum(gx - 1, 0), jnp.minimum(gx + 1, gx_n - 1)
    gym, gyp = jnp.maximum(gy - 1, 0), jnp.minimum(gy + 1, gy_n - 1)

    init_e = remote(rhs_ref.at[subs - 1, 0, :, pl.ds(0, two)], iw, init_send.at[0], init_recv.at[0], gxp, gy)
    init_n = remote(rhs_ref.at[:, 0, :, pl.ds(two, blk)], isou, init_send.at[1], init_recv.at[1], gx, gyp)
    pl.when(has_e)(lambda: init_e.start())
    pl.when(has_n)(lambda: init_n.start())

    total = jnp.int32(0)
    before = jnp.int32(0)

    def count_step(i, carry):
        total, west = carry
        first_tile[i] = total
        east = east_ref[0, i]
        return total + upper_count(west + east + south_n + north_n), east

    total, _ = lax.fori_loop(0, gx_n * subs, count_step, (total, before))
    first_tile[gx_n * subs] = total

    @pl.loop(0, jobs)
    def _(j):
        panel_copy(j).wait()
        tiles[j] = lax.dot_general(
            panels[j, 0], panels[j, 1], (((0,), (0,)), ((), ())), preferred_element_type=F32
        ).astype(BF16)

    def tile_copy(d, i, src):
        return remote(
            send_buf.at[pl.ds(d * cap, cap)], got.at[pl.ds(src * cap, cap)],
            tile_send.at[i], tile_recv.at[i], d, gy,
        )

    def slot_of(d, q):
        slot = (first_tile[d * subs] + gx_n * q - gx + gx_n - 1) // gx_n
        final = (first_tile[d * subs + subs] + gx_n - 1 - gx) // gx_n - 1
        return jnp.clip(jnp.minimum(slot, final), 0, jobs - 1)

    @pl.loop(1, gx_n)
    def _(i):
        d = lax.rem(gx + i, gx_n)
        for q in range(cap):
            send_buf[d * cap + q] = tiles[slot_of(d, q)]
        tile_copy(d, i, gx).start()

    for q in range(cap):
        got[gx * cap + q] = tiles[slot_of(gx, q)]

    lane_w = lax.broadcasted_iota(jnp.int32, (1, two), 1) // blk

    def east_at(i):
        return east_ref[0, gx * subs + i]

    def west_at(i):
        left = east_ref[0, jnp.maximum(gx * subs + i - 1, 0)]
        return left if i > 0 else jnp.where(gx > 0, left, 0)

    masks = []
    for s in range(subs):
        mask_w = (lane_w < west_at(s)).astype(F32)
        mask_e = (lane_w < east_at(s)).astype(F32)
        mask_s = jnp.zeros((1, blk), F32) + south_n.astype(F32)
        mask_n = jnp.zeros((1, blk), F32) + north_n.astype(F32)
        masks.append((mask_w, mask_e, mask_s, mask_n))
    lanes = ((0, two), (two, two), (2 * two, blk), (2 * two + blk, blk))

    center = (CHEB_HIGH + CHEB_LOW) / 2.0
    radius = (CHEB_HIGH - CHEB_LOW) / 2.0
    ratio = center / radius
    rho = 1.0 / ratio

    pl.when(has_w)(lambda: init_e.wait_recv())
    pl.when(has_s)(lambda: init_n.wait_recv())
    pl.when(has_e)(lambda: init_e.wait_send())
    pl.when(has_n)(lambda: init_n.wait_send())
    step = 64

    @pl.loop(0, rows // step)
    def _(c):
        rr = pl.ds(c * step, step)
        for s in range(subs):
            west = -iw[rr, :] if s == 0 else -rhs_ref[s - 1, 0, rr, 0:two]
            parts = (west, rhs_ref[s, 0, rr, 0:two], -isou[s, rr, :], rhs_ref[s, 0, rr, two:two + blk])
            for g, (lo, width) in enumerate(lanes):
                r = parts[g] * masks[s][g]
                u = r / center
                r_ref[s, rr, lo:lo + width] = r
                x_ref[s, rr, lo:lo + width] = u
                xb_ref[s, rr, lo:lo + width] = u.astype(BF16)
                if g == 1:
                    mult_ref[s, 0, rr, 0:two] = u
                if g == 3:
                    mult_ref[s, 0, rr, two:two + blk] = u

    @pl.loop(1, gx_n)
    def _(i):
        copy = tile_copy(lax.rem(gx + i, gx_n), i, gx)
        copy.wait()

    base, end = first_tile[gx * subs], first_tile[gx * subs + subs]
    for s in range(subs):
        west, east = west_at(s), east_at(s)
        nb = west + east + south_n + north_n
        limit = NB - 1
        place = [jnp.int32(0), jnp.int32(1), west, west + 1, west + east, west + east + south_n]
        place = [jnp.minimum(p, limit) for p in place]
        for a in range(NB):
            for b in range(a, NB):
                pa, pb = place[a], place[b]
                k = first_tile[gx * subs + s] + pa * nb - pa * (pa - 1) // 2 + pb - pa
                k = jnp.clip(k, base, end - 1)
                tile = got[lax.rem(k, gx_n) * cap + (k - base) // gx_n]
                mats[s, a * blk:(a + 1) * blk, b * blk:(b + 1) * blk] = tile
                if a < b:
                    mats[s, b * blk:(b + 1) * blk, a * blk:(a + 1) * blk] = tile.T

    part = rows // HALVES

    def product(h, s, g):
        lo, width = lanes[g]
        return jnp.dot(
            xb_ref[s, h * part:(h + 1) * part, :], mats[s, :, lo:lo + width], preferred_element_type=F32
        )

    def halo(t, h):
        sems = lambda g: (face_send.at[t, h, g], face_recv.at[t, h, g])
        to_s = remote(ss.at[t, h], rn.at[t, h], *sems(2), gx, gym), has_s, has_n
        to_w = remote(sw.at[t, h], re.at[t, h], *sems(0), gxm, gy), has_w, has_e
        if t == ITERS - 1:
            return to_s, to_w
        to_n = remote(sn.at[t, h], rs.at[t, h], *sems(3), gx, gyp), has_n, has_s
        to_e = remote(se.at[t, h], rw.at[t, h], *sems(1), gxp, gy), has_e, has_w
        return to_s, to_w, to_n, to_e

    def multiply(t, h):
        copies = halo(t, h)
        last = t == ITERS - 1
        rr = slice(h * part, (h + 1) * part)
        for s in range(subs):
            y = product(h, s, 2)
            y_ref[s, rr, 2 * two:2 * two + blk] = y
            ss[t, h, s] = y.astype(BF16)
        pl.when(has_s)(copies[0][0].start)
        for s in range(subs):
            y = product(h, s, 3)
            y_ref[s, rr, 2 * two + blk:] = y
            if not last:
                sn[t, h, s] = y.astype(BF16)
        if not last:
            pl.when(has_n)(copies[2][0].start)
        y = product(h, 0, 0)
        y_ref[0, rr, 0:two] = y
        sw[t, h] = y.astype(BF16)
        pl.when(has_w)(copies[1][0].start)
        y = product(h, subs - 1, 1)
        y_ref[subs - 1, rr, two:2 * two] = y
        if not last:
            se[t, h] = y.astype(BF16)
            pl.when(has_e)(copies[3][0].start)
        for s in range(subs):
            if s > 0:
                y_ref[s, rr, 0:two] = product(h, s, 0)
            if s < subs - 1:
                y_ref[s, rr, two:2 * two] = product(h, s, 1)

    def advance(t, h, keep, gain):
        last = t == ITERS - 1
        for copy, sends, receives in halo(t, h):
            pl.when(receives)(copy.wait_recv)
            pl.when(sends)(copy.wait_send)

        @pl.loop(0, part // step)
        def _(c):
            ll = pl.ds(c * step, step)
            rr = pl.ds(h * part + c * step, step)
            for s in range(subs):
                for g, (lo, width) in enumerate(lanes):
                    if last and g in (0, 2):
                        continue
                    if g == 0:
                        other = rw[t, h, ll, :].astype(F32) if s == 0 else y_ref[s - 1, rr, two:2 * two]
                    elif g == 1:
                        other = re[t, h, ll, :].astype(F32) if s == subs - 1 else y_ref[s + 1, rr, 0:two]
                    elif g == 2:
                        other = rs[t, h, s, ll, :].astype(F32)
                    else:
                        other = rn[t, h, s, ll, :].astype(F32)
                    y = y_ref[s, rr, lo:lo + width]
                    r = r_ref[s, rr, lo:lo + width] - (y - other) * masks[s][g]
                    olo, ohi = (0, two) if g == 1 else (two, two + blk)
                    if last:
                        res_ref[s, 0, rr, olo:ohi] = r
                        continue
                    u = keep * x_ref[s, rr, lo:lo + width] + gain * r
                    r_ref[s, rr, lo:lo + width] = r
                    x_ref[s, rr, lo:lo + width] = u
                    xb_ref[s, rr, lo:lo + width] = u.astype(BF16)
                    if g in (1, 3):
                        mult_ref[s, 0, rr, olo:ohi] = mult_ref[s, 0, rr, olo:ohi] + u

    for h in range(HALVES):
        multiply(0, h)
    for t in range(ITERS):
        rho_next = 1.0 / (2.0 * ratio - rho)
        keep, gain = rho_next * rho, 2.0 * rho_next / radius
        rho = rho_next
        for h in range(HALVES):
            advance(t, h, keep, gain)
            if t < ITERS - 1:
                multiply(t + 1, h)


def shards(gx_n, gy_n, east_blocks, job_code, factor_panels, dual_rhs):
    jobs = factor_panels.shape[0]
    depth, blk = factor_panels.shape[-2:]
    subs, _, rows, face = dual_rhs.shape
    cap = (subs * upper_count(NB) + gx_n - 1) // gx_n
    width = NB * blk
    vm = pltpu.VMEM
    dma = pltpu.SemaphoreType.DMA
    half = (ITERS, HALVES, rows // HALVES, 2 * blk)
    pair = (ITERS, HALVES, subs, rows // HALVES, blk)
    out = jax.ShapeDtypeStruct(dual_rhs.shape, F32)
    return pl.pallas_call(
        functools.partial(kernel, gx_n, gy_n, jobs, subs, cap, blk),
        out_shape=(out, out),
        in_specs=[
            pl.BlockSpec(memory_space=pltpu.SMEM),
            pl.BlockSpec(memory_space=pl.ANY),
            pl.BlockSpec(memory_space=vm),
        ],
        out_specs=(pl.BlockSpec(memory_space=vm), pl.BlockSpec(memory_space=vm)),
        scratch_shapes=[
            vm((jobs, 2, depth, blk), BF16),
            vm((jobs, blk, blk), BF16),
            vm((gx_n * cap, blk, blk), BF16),
            vm((gx_n * cap, blk, blk), BF16),
            vm((subs, width, width), BF16),
            vm((subs, rows, width), F32),
            vm((subs, rows, width), F32),
            vm((subs, rows, width), F32),
            vm((subs, rows, width), BF16),
            vm(half, BF16), vm(half, BF16), vm(pair, BF16), vm(pair, BF16),
            vm(half, BF16), vm(half, BF16), vm(pair, BF16), vm(pair, BF16),
            vm((rows, 2 * blk), F32),
            vm((subs, rows, blk), F32),
            pltpu.SMEM((gx_n * subs + 1,), jnp.int32),
            dma((jobs,)), dma((gx_n,)), dma((gx_n,)),
            dma((ITERS, HALVES, 4)), dma((ITERS, HALVES, 4)), dma((2,)), dma((2,)),
        ],
        compiler_params=pltpu.CompilerParams(
            collective_id=0, has_side_effects=True, vmem_limit_bytes=56 * 2**20
        ),
    )(east_blocks.T, factor_panels, dual_rhs)


def solution(mesh):
    in_specs = (
        P(None, "gy"),
        P("gx", "gy"),
        P("gx", "gy", None, None, None),
        P("gx", "gy", None, None),
    )
    out_specs = (P("gx", "gy", None, None), P("gx", "gy", None, None))
    body = functools.partial(shards, mesh.shape["gx"], mesh.shape["gy"])
    return jax.shard_map(body, mesh=mesh, in_specs=in_specs, out_specs=out_specs, check_vma=False)
```
